32 devices in a mesh: row: 8 (over y, x, core), col: 4 (over z).
Axes of the slice: x: 2, y: 2, z: 4, core: 2. Of those that a mesh axis runs over, the one named last changes fastest.
Arguments:
- tokens: bfloat16 [512, 8192], P('row', 'col'), may hold values from -6 to 6
- gate_up: bfloat16 [8192, 2, 16384], P('col', None, 'row'), may hold values from -0.0625 to 0.0625
- cotangent: bfloat16 [512, 16384], P('col', 'row'), may hold values from -6 to 6
Outputs:
- hidden: bfloat16 [512, 16384], P('col', 'row')
- input_grad: bfloat16 [512, 8192], P('row', 'col')
- weight_grad: bfloat16 [8192, 2, 16384], P('col', None, 'row')
The draws below stay inside these ranges and needn't reach their ends.
All inputs are finite; a program needn't handle non-finite values.
Results may differ from the reference program's by a relative error of at most 0.0049.
Values may be sent and summed in bfloat16 or wider, within the bound.
A program may use at most 128 MiB of HBM per device.

```python
import jax
import jax.numpy as jnp
from jax import lax

D = 8192
FF = 16384
TOKENS = 512


def raised(result, stream_key, source, target, blocks, factor):
    def block_of(dim):
        return (jnp.arange(result.shape[dim]) // (result.shape[dim] // blocks)).reshape((-1,) + (1,) * (result.ndim - 1 - dim))

    first = jax.random.permutation(stream_key, blocks)[block_of(target)]
    far = (block_of(target) + blocks // 2) % blocks
    return jnp.where((block_of(source) == first) | (block_of(source) == far), factor * result, result)


def block_levels(stream_key, shape, cuts, low, top_value):
    gain, own = 1.0, jax.random.fold_in(stream_key, 6)
    for axis_at, blocks in cuts:
        steps = jnp.exp(jax.random.uniform(jax.random.fold_in(own, axis_at), (blocks,), jnp.float32, low / len(cuts), top_value / len(cuts)))
        gain = gain * jnp.repeat(steps, shape[axis_at] // blocks).reshape([-1 if axis == axis_at else 1 for axis in range(len(shape))])
    return gain


def scatter_about(rng, extent, scale, limit, shards=(), held_as=jnp.bfloat16):
    values = jax.random.normal(rng, extent, jnp.float32) * scale
    if len(shards) > 0:
        values = block_levels(rng, extent, shards, -0.22, 0.18) * values
    return jnp.clip(values, min=-limit, max=limit).astype(held_as)


def heavy_noise(stream_key, shape, spread, reach, cuts, heavy, held_as=jnp.bfloat16):
    values = spread * jax.random.normal(stream_key, shape, jnp.float32)
    if cuts:
        values = values * block_levels(stream_key, shape, cuts, -0.22, 0.18)
    return jnp.clip(raised(values, jax.random.fold_in(stream_key, 3), *heavy), -reach, reach).astype(held_as)


def setup_inputs(seed: int = 0) -> dict:
    splits = jax.random.split(jax.random.key(seed), 4)
    tokens = scatter_about(splits[0], (TOKENS, D), 1.0, 6.0, ((0, 8), (1, 4)))
    gate_up = scatter_about(splits[1], (D, 2, FF), D ** -0.5, 0.0625, ((0, 4), (2, 8)))
    cotangent = heavy_noise(splits[2], (TOKENS, FF), 1.0, 6.0, ((0, 4), (1, 8)), (1, 0, 8, 2.0))
    return {"tokens": tokens, "gate_up": gate_up, "cotangent": cotangent}


def reference(tokens, gate_up, cotangent):
    weights = gate_up.reshape(D, 2 * FF)
    combined = jnp.dot(tokens, weights, preferred_element_type=jnp.float32)
    gate_pre = combined[:, :FF]
    up_pre = combined[:, FF:]
    sigmoid = jax.nn.sigmoid(gate_pre)
    activated = gate_pre * sigmoid
    hidden = (activated * up_pre).astype(jnp.bfloat16)
    grad_out = cotangent.astype(jnp.float32)
    grad_gate = grad_out * up_pre * sigmoid * (1.0 + gate_pre * (1.0 - sigmoid))
    grad_up = grad_out * activated
    stacked = jnp.stack([grad_gate, grad_up], axis=1).astype(jnp.bfloat16)
    flat_grads = stacked.reshape(TOKENS, 2 * FF)
    weight_grad = lax.dot_general(tokens, flat_grads, (((0,), (0,)), ((), ())),
                                  preferred_element_type=jnp.float32)
    weight_grad = weight_grad.astype(jnp.bfloat16).reshape(D, 2, FF)
    input_grad = lax.dot_general(flat_grads, weights, (((1,), (1,)), ((), ())),
                                 preferred_element_type=jnp.float32)
    return hidden, input_grad.astype(jnp.bfloat16), weight_grad
```

```python
import functools

import jax
import jax.numpy as jnp
from jax import lax
from jax.experimental import pallas as pl
from jax.experimental.pallas import tpu as pltpu
from jax.sharding import PartitionSpec as P

MESH = pl.DeviceIdType.MESH


def exchange_kernel(
    n, width, part_ref, cot_ref, hid_ref, g_ref, from_left, from_right, acc,
    rs_send_r, rs_recv_r, rs_send_l, rs_recv_l, ag_send_r, ag_send_l, ag_recv,
):
    p = lax.axis_index("col")
    rows = cot_ref.shape[0]
    hidden = cot_ref.shape[1]
    chunks = hidden // width
    has_left, has_right = p > 0, p < n - 1

    def place(c, b):
        return (
            slice(None),
            pl.ds(pl.multiple_of(b * rows, rows), rows),
            pl.ds(pl.multiple_of(c * width, width), width),
        )

    def own_part(c, b, k):
        return part_ref[
            pl.ds(pl.multiple_of(b * rows, rows), rows),
            pl.ds(pl.multiple_of(k * hidden + c * width, width), width),
        ]

    def copy(src, dst, send, recv, target):
        return pltpu.make_async_remote_copy(
            src_ref=src, dst_ref=dst, send_sem=send, recv_sem=recv,
            device_id={"col": target}, device_id_type=MESH,
        )

    def rs_right(c, b):
        at = from_left.at[place(c, b)]
        return copy(at, at, rs_send_r.at[c, b], rs_recv_r.at[c, b], p + 1)

    def rs_left(c, b):
        at = from_right.at[place(c, b)]
        return copy(at, at, rs_send_l.at[c, b], rs_recv_l.at[c, b], p - 1)

    def ag_right(c, b):
        at = g_ref.at[place(c, b)]
        return copy(at, at, ag_send_r.at[c, b], ag_recv.at[c, b], p + 1)

    def ag_left(c, b):
        at = g_ref.at[place(c, b)]
        return copy(at, at, ag_send_l.at[c, b], ag_recv.at[c, b], p - 1)

    def relay(c, b, buffer, descriptor, arrives):
        _, at_rows, at_cols = place(c, b)

        @pl.when(arrives)
        def _():
            descriptor(c, b).wait_recv()
            for k in range(2):
                total = own_part(c, b, k) + buffer[k, at_rows, at_cols].astype(jnp.float32)
                buffer[k, at_rows, at_cols] = total.astype(buffer.dtype)

        @pl.when(jnp.logical_not(arrives))
        def _():
            for k in range(2):
                buffer[k, at_rows, at_cols] = own_part(c, b, k).astype(buffer.dtype)

        descriptor(c, b).start()

    def relay_right(c):
        for b in range(n - 1, 0, -1):
            pl.when(p < b)(functools.partial(relay, c, b, from_left, rs_right, has_left))

    def relay_left(c):
        for b in range(n - 1):
            pl.when(p > b)(functools.partial(relay, c, b, from_right, rs_left, has_right))

    def reduce(c):
        @pl.when(2 * p < n)
        def _():
            relay_right(c)
            relay_left(c)

        @pl.when(2 * p >= n)
        def _():
            relay_left(c)
            relay_right(c)

    def finish(c):
        _, at_rows, at_cols = place(c, p)
        for k in range(2):
            acc[k] = own_part(c, p, k)

        @pl.when(has_left)
        def _():
            rs_right(c, p).wait_recv()
            for k in range(2):
                acc[k] += from_left[k, at_rows, at_cols].astype(jnp.float32)

        @pl.when(has_right)
        def _():
            rs_left(c, p).wait_recv()
            for k in range(2):
                acc[k] += from_right[k, at_rows, at_cols].astype(jnp.float32)

        gate_pre, up_pre = acc[0], acc[1]
        sigmoid = jax.nn.sigmoid(gate_pre)
        activated = gate_pre * sigmoid
        grad_out = cot_ref[:, at_cols].astype(jnp.float32)
        hid_ref[:, at_cols] = (activated * up_pre).astype(hid_ref.dtype)
        grad_gate = grad_out * up_pre * sigmoid * (1.0 + gate_pre * (1.0 - sigmoid))
        g_ref[0, at_rows, at_cols] = grad_gate.astype(g_ref.dtype)
        g_ref[1, at_rows, at_cols] = (grad_out * activated).astype(g_ref.dtype)

        @pl.when(has_right)
        def _():
            ag_right(c, p).start()

        @pl.when(has_left)
        def _():
            ag_left(c, p).start()

    def spread(c):
        for d in range(1, n):

            @pl.when(p >= d)
            def _():
                ag_right(c, p - d).wait_recv()

                @pl.when(has_right)
                def _():
                    ag_right(c, p - d).start()

            @pl.when(p + d < n)
            def _():
                ag_left(c, p + d).wait_recv()

                @pl.when(has_left)
                def _():
                    ag_left(c, p + d).start()

    barrier = pltpu.get_barrier_semaphore()
    for here, step in ((has_left, -1), (has_right, 1)):

        @pl.when(here)
        def _():
            pl.semaphore_signal(barrier, inc=1, device_id={"col": p + step}, device_id_type=MESH)

    pl.semaphore_wait(barrier, has_left.astype(jnp.int32) + has_right.astype(jnp.int32))

    def step(i, carry):
        pl.when(i < chunks)(lambda: reduce(i))
        pl.when(jnp.logical_and(i >= 1, i < chunks + 1))(lambda: finish(i - 1))
        pl.when(i >= 2)(lambda: spread(i - 2))
        return carry

    lax.fori_loop(0, chunks + 2, step, 0)

    def drain(c, carry):
        for b in range(n):
            pl.when(p < b)(lambda: rs_right(c, b).wait_send())
            pl.when(p > b)(lambda: rs_left(c, b).wait_send())
            pl.when(jnp.logical_and(has_right, p >= b))(lambda: ag_right(c, b).wait_send())
            pl.when(jnp.logical_and(has_left, p <= b))(lambda: ag_left(c, b).wait_send())
        return carry

    lax.fori_loop(0, chunks, drain, 0)


def exchange(part, cotangent, n):
    rows, hidden = cotangent.shape
    total_rows = part.shape[0]
    width = min(256, hidden)
    chunks = hidden // width
    vmem = pl.BlockSpec(memory_space=pltpu.VMEM)
    sem = pltpu.SemaphoreType.DMA((chunks, n))
    held = pltpu.VMEM((2, total_rows, hidden), jnp.bfloat16)
    return pl.pallas_call(
        functools.partial(exchange_kernel, n, width),
        out_shape=(
            jax.ShapeDtypeStruct((rows, hidden), jnp.bfloat16),
            jax.ShapeDtypeStruct((2, total_rows, hidden), jnp.bfloat16),
        ),
        in_specs=[vmem, vmem],
        out_specs=(vmem, vmem),
        scratch_shapes=[held, held, pltpu.VMEM((2, rows, width), jnp.float32)] + [sem] * 7,
        compiler_params=pltpu.CompilerParams(
            collective_id=0, has_side_effects=True, vmem_limit_bytes=48 * 2**20
        ),
    )(part, cotangent)


def on_device(n_col, tokens, gate_up, cotangent):
    local_feats = tokens.shape[1]
    local_hidden = gate_up.shape[2]
    gathered = lax.all_gather(tokens, "row", axis=0, tiled=True)
    weights = gate_up.reshape(local_feats, 2 * local_hidden)
    part = jnp.dot(gathered, weights, preferred_element_type=jnp.float32)
    hidden, grads = exchange(part, cotangent, n_col)
    flat = jnp.concatenate([grads[0], grads[1]], axis=1)
    input_grad = lax.psum_scatter(
        lax.dot_general(
            flat, weights, (((1,), (1,)), ((), ())), preferred_element_type=jnp.float32
        ),
        "row",
        scatter_dimension=0,
        tiled=True,
    ).astype(jnp.bfloat16)
    weight_grad = jnp.stack(
        [
            lax.dot_general(
                gathered, grads[k], (((0,), (0,)), ((), ())), preferred_element_type=jnp.float32
            ).astype(jnp.bfloat16)
            for k in range(2)
        ],
        axis=1,
    )
    return (hidden, input_grad, weight_grad)


def solution(mesh):
    in_specs = (P("row", "col"), P("col", None, "row"), P("col", "row"))
    out_specs = (P("col", "row"), P("row", "col"), P("col", None, "row"))
    return jax.shard_map(
        functools.partial(on_device, mesh.shape["col"]),
        mesh=mesh, in_specs=in_specs, out_specs=out_specs, check_vma=False,
    )
```

```python
import functools

import jax
import jax.numpy as jnp
from jax import lax
from jax.experimental import pallas as pl
from jax.experimental.pallas import tpu as pltpu
from jax.sharding import PartitionSpec as P

MESH = pl.DeviceIdType.MESH


def exchange_kernel(
    n, unit_rows, width, part_ref, cot_ref, hid_ref, g_ref, from_left, from_right, acc,
    rs_send_r, rs_recv_r, rs_send_l, rs_recv_l, ag_send_r, ag_send_l, ag_recv,
):
    p = lax.axis_index("col")
    rows, hidden = cot_ref.shape
    cuts = rows // unit_rows
    units = cuts * (hidden // width)
    has_left, has_right = p > 0, p < n - 1

    def rows_of(u, b):
        return pl.ds(pl.multiple_of(b * rows + (u % cuts) * unit_rows, unit_rows), unit_rows)

    def cols_of(u, k=0):
        return pl.ds(pl.multiple_of(k * hidden + (u // cuts) * width, width), width)

    def own_part(u, b, k):
        return part_ref[rows_of(u, b), cols_of(u, k)]

    def copy(at, send, recv, target):
        return pltpu.make_async_remote_copy(
            src_ref=at, dst_ref=at, send_sem=send, recv_sem=recv,
            device_id={"col": target}, device_id_type=MESH,
        )

    def rs_right(u, b):
        return copy(from_left.at[u, b], rs_send_r.at[u, b], rs_recv_r.at[u, b], p + 1)

    def rs_left(u, b):
        return copy(from_right.at[u, b], rs_send_l.at[u, b], rs_recv_l.at[u, b], p - 1)

    def ag_right(u, b):
        at = g_ref.at[:, rows_of(u, b), cols_of(u)]
        return copy(at, ag_send_r.at[u, b], ag_recv.at[u, b], p + 1)

    def ag_left(u, b):
        at = g_ref.at[:, rows_of(u, b), cols_of(u)]
        return copy(at, ag_send_l.at[u, b], ag_recv.at[u, b], p - 1)

    def when_unit(u, more, body):
        pl.when(jnp.logical_and(jnp.logical_and(u >= 0, u < units), more))(body)

    def relay(u, b, buffer, descriptor, arrives):
        @pl.when(arrives)
        def _():
            descriptor(u, b).wait_recv()
            for k in range(2):
                total = own_part(u, b, k) + buffer[u, b, k].astype(jnp.float32)
                buffer[u, b, k] = total.astype(buffer.dtype)

        @pl.when(jnp.logical_not(arrives))
        def _():
            for k in range(2):
                buffer[u, b, k] = own_part(u, b, k).astype(buffer.dtype)

        descriptor(u, b).start()

    def finish(u):
        for k in range(2):
            acc[k] = own_part(u, p, k)

        @pl.when(has_left)
        def _():
            rs_right(u, p).wait_recv()
            for k in range(2):
                acc[k] += from_left[u, p, k].astype(jnp.float32)

        @pl.when(has_right)
        def _():
            rs_left(u, p).wait_recv()
            for k in range(2):
                acc[k] += from_right[u, p, k].astype(jnp.float32)

        gate_pre, up_pre = acc[0], acc[1]
        sigmoid = jax.nn.sigmoid(gate_pre)
        activated = gate_pre * sigmoid
        here, at_rows, at_cols = rows_of(u, 0), rows_of(u, p), cols_of(u)
        grad_out = cot_ref[here, at_cols].astype(jnp.float32)
        hid_ref[here, at_cols] = (activated * up_pre).astype(hid_ref.dtype)
        grad_gate = grad_out * up_pre * sigmoid * (1.0 + gate_pre * (1.0 - sigmoid))
        g_ref[0, at_rows, at_cols] = grad_gate.astype(g_ref.dtype)
        g_ref[1, at_rows, at_cols] = (grad_out * activated).astype(g_ref.dtype)

        @pl.when(has_right)
        def _():
            ag_right(u, p).start()

        @pl.when(has_left)
        def _():
            ag_left(u, p).start()

    def forward_right(u, b):
        ag_right(u, b).wait_recv()
        pl.when(has_right)(lambda: ag_right(u, b).start())

    def forward_left(u, b):
        ag_left(u, b).wait_recv()
        pl.when(has_left)(lambda: ag_left(u, b).start())

    barrier = pltpu.get_barrier_semaphore()
    for here, step in ((has_left, -1), (has_right, 1)):

        @pl.when(here)
        def _():
            pl.semaphore_signal(barrier, inc=1, device_id={"col": p + step}, device_id_type=MESH)

    pl.semaphore_wait(barrier, has_left.astype(jnp.int32) + has_right.astype(jnp.int32))

    def iteration(i, carry):
        for s in range(n - 1):
            b = n - 1 - s
            when_unit(
                i - p, p < b,
                functools.partial(relay, i - p, b, from_left, rs_right, has_left),
            )
            when_unit(
                i - (n - 1 - p), p > s,
                functools.partial(relay, i - (n - 1 - p), s, from_right, rs_left, has_right),
            )
        summed = i - jnp.maximum(p, n - 1 - p)
        when_unit(summed, True, functools.partial(finish, summed))
        for b in range(n):
            lag = max(b, n - 1 - b)
            u = i - lag - (p - b)
            when_unit(u, p > b, functools.partial(forward_right, u, b))
            u = i - lag - (b - p)
            when_unit(u, p < b, functools.partial(forward_left, u, b))
        return carry

    lax.fori_loop(0, units + 2 * (n - 1), iteration, 0)

    def drain(u, carry):
        for b in range(n):
            pl.when(p < b)(lambda: rs_right(u, b).wait_send())
            pl.when(p > b)(lambda: rs_left(u, b).wait_send())
            pl.when(jnp.logical_and(has_right, p >= b))(lambda: ag_right(u, b).wait_send())
            pl.when(jnp.logical_and(has_left, p <= b))(lambda: ag_left(u, b).wait_send())
        return carry

    lax.fori_loop(0, units, drain, 0)


def exchange(part, cotangent, n):
    rows, hidden = cotangent.shape
    total_rows = part.shape[0]
    unit_rows, width = 64, 128
    units = (rows // unit_rows) * (hidden // width)
    vmem = pl.BlockSpec(memory_space=pltpu.VMEM)
    sem = pltpu.SemaphoreType.DMA((units, n))
    held = pltpu.VMEM((units, n, 2, unit_rows, width), jnp.bfloat16)
    return pl.pallas_call(
        functools.partial(exchange_kernel, n, unit_rows, width),
        out_shape=(
            jax.ShapeDtypeStruct((rows, hidden), jnp.bfloat16),
            jax.ShapeDtypeStruct((2, total_rows, hidden), jnp.bfloat16),
        ),
        in_specs=[vmem, vmem],
        out_specs=(vmem, vmem),
        scratch_shapes=[held, held, pltpu.VMEM((2, unit_rows, width), jnp.float32)] + [sem] * 7,
        compiler_params=pltpu.CompilerParams(
            collective_id=0, has_side_effects=True, vmem_limit_bytes=48 * 2**20
        ),
    )(part, cotangent)


def tail_kernel(
    n, tile, part_ref, tok_ref, g_ref, in_grad_ref, w_grad_ref, acc, sent, got, tiles,
    send_sem, recv_sem, out_sem,
):
    r = lax.axis_index("row")
    bits = n.bit_length() - 1
    rows, feats = in_grad_ref.shape
    half = feats // 2
    orders = (tuple(range(bits)), (0,) + tuple(range(bits - 1, 0, -1)))

    def own(bit):
        return (r // 2**bit) % 2

    def partner(bit):
        return r + (1 - 2 * own(bit)) * 2**bit

    def block(order, stage, e, keep):
        at = 0
        for bit in order[:stage]:
            at = at + own(bit) * 2**bit
        bit = order[stage]
        at = at + (own(bit) if keep else 1 - own(bit)) * 2**bit
        for place, bit in enumerate(order[stage + 1 :]):
            at = at + ((e >> place) & 1) * 2**bit
        return at

    def slots(stage):
        count = n >> (stage + 1)
        first = n - (n >> stage)
        return [(e, first + e) for e in range(count)]

    def copy(h, stage, slot):
        return pltpu.make_async_remote_copy(
            src_ref=sent.at[h, slot], dst_ref=got.at[h, slot],
            send_sem=send_sem.at[h, slot], recv_sem=recv_sem.at[h, slot],
            device_id={"row": partner(orders[h][stage])}, device_id_type=MESH,
        )

    def send(stage):
        for h in range(2):
            for e, slot in slots(stage):
                b = block(orders[h], stage, e, False)
                value = (part_ref if stage == 0 else acc)[
                    pl.ds(pl.multiple_of(b * rows, rows), rows), h * half : (h + 1) * half
                ]
                sent[h, slot] = value.astype(sent.dtype)
                copy(h, stage, slot).start()

    def receive(stage):
        for h in range(2):
            for e, slot in slots(stage):
                copy(h, stage, slot).wait_recv()
                b = block(orders[h], stage, e, True)
                at = (pl.ds(pl.multiple_of(b * rows, rows), rows), slice(h * half, (h + 1) * half))
                total = (part_ref if stage == 0 else acc)[at] + got[h, slot].astype(jnp.float32)
                if stage == bits - 1:
                    in_grad_ref[:, h * half : (h + 1) * half] = total.astype(in_grad_ref.dtype)
                else:
                    acc[at] = total

    across = feats // tile
    count = 2 * across

    def out_copy(t):
        return pltpu.make_async_copy(
            tiles.at[t % 2],
            w_grad_ref.at[t // across, pl.ds(pl.multiple_of((t % across) * tile, tile), tile)],
            out_sem.at[t % 2],
        )

    def weight_tile(t, carry):
        pl.when(t >= 2)(lambda: out_copy(t - 2).wait())
        cols = pl.ds(pl.multiple_of((t % across) * tile, tile), tile)
        tiles[t % 2] = lax.dot_general(
            tok_ref[:, cols], g_ref[t // across], (((0,), (0,)), ((), ())),
            preferred_element_type=jnp.float32,
        ).astype(tiles.dtype)
        out_copy(t).start()
        return carry

    barrier = pltpu.get_barrier_semaphore()
    for bit in range(bits):
        pl.semaphore_signal(barrier, inc=1, device_id={"row": partner(bit)}, device_id_type=MESH)
    pl.semaphore_wait(barrier, bits)

    shares = 2 * bits - 1
    done = 0
    for stage in range(bits):
        send(stage)
        until = count * (2 * stage + 1) // shares
        lax.fori_loop(done, until, weight_tile, 0)
        done = until
        receive(stage)
    for t in range(count - 2, count):
        out_copy(t).wait()
    for stage in range(bits):
        for h in range(2):
            for _, slot in slots(stage):
                copy(h, stage, slot).wait_send()


def tail(part, gathered, grads, n):
    total_rows, feats = part.shape
    hidden = grads.shape[2]
    rows = total_rows // n
    tile = 256
    vmem = pl.BlockSpec(memory_space=pltpu.VMEM)
    sem = pltpu.SemaphoreType.DMA((2, n - 1))
    held = pltpu.VMEM((2, n - 1, rows, feats // 2), jnp.bfloat16)
    return pl.pallas_call(
        functools.partial(tail_kernel, n, tile),
        out_shape=(
            jax.ShapeDtypeStruct((rows, feats), jnp.bfloat16),
            jax.ShapeDtypeStruct((2, feats, hidden), jnp.bfloat16),
        ),
        in_specs=[vmem, vmem, vmem],
        out_specs=(vmem, pl.BlockSpec(memory_space=pl.ANY)),
        scratch_shapes=[
            pltpu.VMEM((total_rows, feats), jnp.float32), held, held,
            pltpu.VMEM((2, tile, hidden), jnp.bfloat16),
            sem, sem, pltpu.SemaphoreType.DMA((2,)),
        ],
        compiler_params=pltpu.CompilerParams(
            collective_id=1, has_side_effects=True, vmem_limit_bytes=48 * 2**20
        ),
    )(part, gathered, grads)


def on_device(n_row, n_col, tokens, gate_up, cotangent):
    local_feats = tokens.shape[1]
    local_hidden = gate_up.shape[2]
    gathered = lax.all_gather(tokens, "row", axis=0, tiled=True)
    weights = gate_up.reshape(local_feats, 2 * local_hidden)
    part = jnp.dot(gathered, weights, preferred_element_type=jnp.float32)
    hidden, grads = exchange(part, cotangent, n_col)
    flat = jnp.concatenate([grads[0], grads[1]], axis=1)
    in_part = lax.dot_general(
        flat, weights, (((1,), (1,)), ((), ())), preferred_element_type=jnp.float32
    )
    input_grad, weight_grad = tail(in_part, gathered, grads, n_row)
    return (hidden, input_grad, jnp.transpose(weight_grad, (1, 0, 2)))


def solution(mesh):
    in_specs = (P("row", "col"), P("col", None, "row"), P("col", "row"))
    out_specs = (P("col", "row"), P("row", "col"), P("col", None, "row"))
    return jax.shard_map(
        functools.partial(on_device, mesh.shape["row"], mesh.shape["col"]),
        mesh=mesh, in_specs=in_specs, out_specs=out_specs, check_vma=False,
    )
```

```python
import functools

import jax
import jax.numpy as jnp
from jax import lax
from jax.experimental import pallas as pl
from jax.experimental.layout import Layout, with_layout_constraint
from jax.experimental.pallas import tpu as pltpu
from jax.sharding import PartitionSpec as P

MESH = pl.DeviceIdType.MESH


def exchange_kernel(
    n, unit_rows, width, group, tok_ref, w_ref, cot_ref, hid_ref, in_part_ref, w_grad_ref,
    weights, tok_t, part_ref, g_ref, from_left, from_right, acc, tiles,
    rs_send_r, rs_recv_r, rs_send_l, rs_recv_l, ag_send_r, ag_send_l, ag_recv, w_sem, out_sem,
):
    p = lax.axis_index("col")
    rows, hidden = cot_ref.shape
    cuts = rows // unit_rows
    units = cuts * (hidden // width)
    total_rows, feats = tok_ref.shape
    groups, steps = hidden // group, cuts * group // width
    halves = steps // 2
    lag_max = 2 * (n - 1)
    has_left, has_right = p > 0, p < n - 1

    def rows_of(u, b):
        return pl.ds(pl.multiple_of(b * rows + (u % cuts) * unit_rows, unit_rows), unit_rows)

    def cols_of(u, k=0):
        return pl.ds(pl.multiple_of(k * hidden + (u // cuts) * width, width), width)

    def own_part(u, b, k):
        return part_ref[rows_of(u, b), cols_of(u, k)]

    def copy(at, send, recv, target):
        return pltpu.make_async_remote_copy(
            src_ref=at, dst_ref=at, send_sem=send, recv_sem=recv,
            device_id={"col": target}, device_id_type=MESH,
        )

    def rs_right(u, b):
        return copy(from_left.at[u, b], rs_send_r.at[u, b], rs_recv_r.at[u, b], p + 1)

    def rs_left(u, b):
        return copy(from_right.at[u, b], rs_send_l.at[u, b], rs_recv_l.at[u, b], p - 1)

    def ag_right(u, b):
        at = g_ref.at[:, rows_of(u, b), cols_of(u)]
        return copy(at, ag_send_r.at[u, b], ag_recv.at[u, b], p + 1)

    def ag_left(u, b):
        at = g_ref.at[:, rows_of(u, b), cols_of(u)]
        return copy(at, ag_send_l.at[u, b], ag_recv.at[u, b], p - 1)

    def when_unit(u, more, body):
        pl.when(jnp.logical_and(jnp.logical_and(u >= 0, u < units), more))(body)

    def relay(u, b, buffer, descriptor, arrives):
        @pl.when(arrives)
        def _():
            descriptor(u, b).wait_recv()
            for k in range(2):
                total = own_part(u, b, k) + buffer[u, b, k].astype(jnp.float32)
                buffer[u, b, k] = total.astype(buffer.dtype)

        @pl.when(jnp.logical_not(arrives))
        def _():
            for k in range(2):
                buffer[u, b, k] = own_part(u, b, k).astype(buffer.dtype)

        descriptor(u, b).start()

    def finish(u):
        for k in range(2):
            acc[k] = own_part(u, p, k)

        @pl.when(has_left)
        def _():
            rs_right(u, p).wait_recv()
            for k in range(2):
                acc[k] += from_left[u, p, k].astype(jnp.float32)

        @pl.when(has_right)
        def _():
            rs_left(u, p).wait_recv()
            for k in range(2):
                acc[k] += from_right[u, p, k].astype(jnp.float32)

        gate_pre, up_pre = acc[0], acc[1]
        sigmoid = jax.nn.sigmoid(gate_pre)
        activated = gate_pre * sigmoid
        here, at_rows, at_cols = rows_of(u, 0), rows_of(u, p), cols_of(u)
        grad_out = cot_ref[here, at_cols].astype(jnp.float32)
        hid_ref[here, at_cols] = (activated * up_pre).astype(hid_ref.dtype)
        grad_gate = grad_out * up_pre * sigmoid * (1.0 + gate_pre * (1.0 - sigmoid))
        g_ref[0, at_rows, at_cols] = grad_gate.astype(g_ref.dtype)
        g_ref[1, at_rows, at_cols] = (grad_out * activated).astype(g_ref.dtype)

        @pl.when(has_right)
        def _():
            ag_right(u, p).start()

        @pl.when(has_left)
        def _():
            ag_left(u, p).start()

    def forward_right(u, b):
        ag_right(u, b).wait_recv()
        pl.when(has_right)(lambda: ag_right(u, b).start())

    def forward_left(u, b):
        ag_left(u, b).wait_recv()
        pl.when(has_left)(lambda: ag_left(u, b).start())

    barrier = pltpu.get_barrier_semaphore()
    for here, step in ((has_left, -1), (has_right, 1)):

        @pl.when(here)
        def _():
            pl.semaphore_signal(barrier, inc=1, device_id={"col": p + step}, device_id_type=MESH)

    def weight_copy(q, k):
        return pltpu.make_async_copy(
            w_ref.at[:, pl.ds(pl.multiple_of(k * hidden + q * group, group), group)],
            weights.at[q, k], w_sem.at[q, k],
        )

    def group_cols(q, k=0):
        return pl.ds(pl.multiple_of(k * hidden + q * group, group), group)

    def piece(j, size):
        return pl.ds(pl.multiple_of(j * size, size), size)

    def forward_step(q, j):
        @pl.when(j == 0)
        def _():
            weight_copy(q, 0).wait()
            weight_copy(q, 1).wait()

        k, at = j // halves, piece(j % halves, total_rows // halves)
        part_ref[at, group_cols(q, k)] = jnp.dot(
            tok_ref[at, :], weights[q, k], preferred_element_type=jnp.float32
        )

    def out_copy(t):
        j = t % steps
        size = feats // halves // 16
        return pltpu.make_async_copy(
            tiles.at[t % 2],
            w_grad_ref.at[piece(j % halves, size), j // halves, :, group_cols(t // steps)],
            out_sem.at[t % 2],
        )

    def backward_step(t):
        q, j = t // steps, t % steps
        at = piece(j, total_rows // steps)
        in_part_ref[at, :] += sum(
            lax.dot_general(
                g_ref[k, at, group_cols(q)], weights[q, k], (((1,), (1,)), ((), ())),
                preferred_element_type=jnp.float32,
            )
            for k in range(2)
        )
        pl.when(t >= 2)(lambda: out_copy(t - 2).wait())
        tile = jnp.dot(
            tok_t[piece(j % halves, feats // halves), :], g_ref[j // halves, :, group_cols(q)],
            preferred_element_type=jnp.float32,
        )
        tiles[t % 2] = tile.astype(tiles.dtype).reshape(tiles.shape[1:])
        out_copy(t).start()

    for q in range(groups):
        for k in range(2):
            weight_copy(q, k).start()
    in_part_ref[...] = jnp.zeros_like(in_part_ref)

    def turn(j, carry):
        at = piece(j, group)
        tok_t[at, :] = tok_ref[:, at].T
        return carry

    lax.fori_loop(0, feats // group, turn, 0)

    def first(j, carry):
        forward_step(0, j)
        return carry

    lax.fori_loop(0, steps, first, 0)
    pl.semaphore_wait(barrier, has_left.astype(jnp.int32) + has_right.astype(jnp.int32))

    def iteration(i, carry):
        for s in range(n - 1):
            b = n - 1 - s
            when_unit(
                i - p, p < b,
                functools.partial(relay, i - p, b, from_left, rs_right, has_left),
            )
            when_unit(
                i - (n - 1 - p), p > s,
                functools.partial(relay, i - (n - 1 - p), s, from_right, rs_left, has_right),
            )
        summed = i - jnp.maximum(p, n - 1 - p)
        when_unit(summed, True, functools.partial(finish, summed))
        for b in range(n):
            lag = max(b, n - 1 - b)
            u = i - lag - (p - b)
            when_unit(u, p > b, functools.partial(forward_right, u, b))
            u = i - lag - (b - p)
            when_unit(u, p < b, functools.partial(forward_left, u, b))
        pl.when(i + steps < units)(lambda: forward_step(i // steps + 1, i % steps))
        pl.when(i >= lag_max + steps)(lambda: backward_step(i - lag_max - steps))
        return carry

    lax.fori_loop(0, units + lag_max + steps, iteration, 0)
    for t in range(units - 2, units):
        out_copy(t).wait()

    def drain(u, carry):
        for b in range(n):
            pl.when(p < b)(lambda: rs_right(u, b).wait_send())
            pl.when(p > b)(lambda: rs_left(u, b).wait_send())
            pl.when(jnp.logical_and(has_right, p >= b))(lambda: ag_right(u, b).wait_send())
            pl.when(jnp.logical_and(has_left, p <= b))(lambda: ag_left(u, b).wait_send())
        return carry

    lax.fori_loop(0, units, drain, 0)


def exchange(gathered, weights, cotangent, n):
    rows, hidden = cotangent.shape
    total_rows, feats = gathered.shape
    unit_rows, width, group = 64, 128, 256
    units = (rows // unit_rows) * (hidden // width)
    steps = (rows // unit_rows) * (group // width)
    vmem = pl.BlockSpec(memory_space=pltpu.VMEM)
    hbm = pl.BlockSpec(memory_space=pl.ANY)
    sem = pltpu.SemaphoreType.DMA((units, n))
    held = pltpu.VMEM((units, n, 2, unit_rows, width), jnp.bfloat16)
    return pl.pallas_call(
        functools.partial(exchange_kernel, n, unit_rows, width, group),
        out_shape=(
            jax.ShapeDtypeStruct((rows, hidden), jnp.bfloat16),
            jax.ShapeDtypeStruct((total_rows, feats), jnp.float32),
            jax.ShapeDtypeStruct((feats // 16, 2, 16, hidden), jnp.bfloat16),
        ),
        in_specs=[vmem, hbm, vmem],
        out_specs=(vmem, vmem, hbm),
        scratch_shapes=[
            pltpu.VMEM((hidden // group, 2, feats, group), jnp.bfloat16),
            pltpu.VMEM((feats, total_rows), jnp.bfloat16),
            pltpu.VMEM((total_rows, 2 * hidden), jnp.float32),
            pltpu.VMEM((2, total_rows, hidden), jnp.bfloat16),
            held, held, pltpu.VMEM((2, unit_rows, width), jnp.float32),
            pltpu.VMEM((2, feats * 2 // steps // 16, 16, group), jnp.bfloat16),
        ]
        + [sem] * 7
        + [pltpu.SemaphoreType.DMA((hidden // group, 2)), pltpu.SemaphoreType.DMA((2,))],
        compiler_params=pltpu.CompilerParams(
            collective_id=0, has_side_effects=True, vmem_limit_bytes=58 * 2**20
        ),
    )(gathered, weights, cotangent)


def tail_kernel(n, part_ref, in_grad_ref, acc, sent, got, send_sem, recv_sem):
    r = lax.axis_index("row")
    bits = n.bit_length() - 1
    rows, feats = in_grad_ref.shape
    half = feats // 2
    orders = (tuple(range(bits)), (0,) + tuple(range(bits - 1, 0, -1)))

    def own(bit):
        return (r // 2**bit) % 2

    def partner(bit):
        return r + (1 - 2 * own(bit)) * 2**bit

    def block(order, stage, e, keep):
        at = 0
        for bit in order[:stage]:
            at = at + own(bit) * 2**bit
        bit = order[stage]
        at = at + (own(bit) if keep else 1 - own(bit)) * 2**bit
        for place, bit in enumerate(order[stage + 1 :]):
            at = at + ((e >> place) & 1) * 2**bit
        return at

    def slots(stage):
        count = n >> (stage + 1)
        first = n - (n >> stage)
        return [(e, first + e) for e in range(count)]

    def copy(h, stage, slot):
        return pltpu.make_async_remote_copy(
            src_ref=sent.at[h, slot], dst_ref=got.at[h, slot],
            send_sem=send_sem.at[h, slot], recv_sem=recv_sem.at[h, slot],
            device_id={"row": partner(orders[h][stage])}, device_id_type=MESH,
        )

    def send(stage):
        for h in range(2):
            for e, slot in slots(stage):
                b = block(orders[h], stage, e, False)
                value = (part_ref if stage == 0 else acc)[
                    pl.ds(pl.multiple_of(b * rows, rows), rows), h * half : (h + 1) * half
                ]
                sent[h, slot] = value.astype(sent.dtype)
                copy(h, stage, slot).start()

    def receive(stage):
        for h in range(2):
            for e, slot in slots(stage):
                copy(h, stage, slot).wait_recv()
                b = block(orders[h], stage, e, True)
                at = (pl.ds(pl.multiple_of(b * rows, rows), rows), slice(h * half, (h + 1) * half))
                total = (part_ref if stage == 0 else acc)[at] + got[h, slot].astype(jnp.float32)
                if stage == bits - 1:
                    in_grad_ref[:, h * half : (h + 1) * half] = total.astype(in_grad_ref.dtype)
                else:
                    acc[at] = total

    barrier = pltpu.get_barrier_semaphore()
    for bit in range(bits):
        pl.semaphore_signal(barrier, inc=1, device_id={"row": partner(bit)}, device_id_type=MESH)
    pl.semaphore_wait(barrier, bits)

    for stage in range(bits):
        send(stage)
        receive(stage)
    for stage in range(bits):
        for h in range(2):
            for _, slot in slots(stage):
                copy(h, stage, slot).wait_send()


def tail(part, n):
    total_rows, feats = part.shape
    rows = total_rows // n
    vmem = pl.BlockSpec(memory_space=pltpu.VMEM)
    sem = pltpu.SemaphoreType.DMA((2, n - 1))
    held = pltpu.VMEM((2, n - 1, rows, feats // 2), jnp.bfloat16)
    return pl.pallas_call(
        functools.partial(tail_kernel, n),
        out_shape=jax.ShapeDtypeStruct((rows, feats), jnp.bfloat16),
        in_specs=[vmem],
        out_specs=vmem,
        scratch_shapes=[pltpu.VMEM((total_rows, feats), jnp.float32), held, held, sem, sem],
        compiler_params=pltpu.CompilerParams(
            collective_id=1, has_side_effects=True, vmem_limit_bytes=48 * 2**20
        ),
    )(part)


def on_device(n_row, n_col, tokens, gate_up, cotangent):
    local_feats = tokens.shape[1]
    local_hidden = gate_up.shape[2]
    gathered = lax.all_gather(tokens, "row", axis=0, tiled=True)
    weights = gate_up.reshape(local_feats, 2 * local_hidden)
    hidden, in_part, weight_grad = exchange(gathered, weights, cotangent, n_col)
    input_grad = tail(in_part, n_row)
    weight_grad = with_layout_constraint(
        jnp.transpose(weight_grad, (0, 2, 1, 3)), Layout(major_to_minor=(0, 1, 2, 3))
    )
    weight_grad = weight_grad.reshape(gate_up.shape)
    return (hidden, input_grad, weight_grad)


def solution(mesh):
    in_specs = (P("row", "col"), P("col", None, "row"), P("col", "row"))
    out_specs = (P("col", "row"), P("row", "col"), P("col", None, "row"))
    return jax.shard_map(
        functools.partial(on_device, mesh.shape["row"], mesh.shape["col"]),
        mesh=mesh, in_specs=in_specs, out_specs=out_specs, check_vma=False,
    )
```

```python
import functools

import jax
import jax.numpy as jnp
from jax import lax
from jax.experimental import pallas as pl
from jax.experimental.layout import Layout, with_layout_constraint
from jax.experimental.pallas import tpu as pltpu
from jax.sharding import PartitionSpec as P

MESH = pl.DeviceIdType.MESH


def exchange_kernel(
    n, unit_rows, width, group, tok_ref, w_ref, cot_ref, hid_ref, in_part_ref, w_grad_ref,
    weights, tok_t, part_ref, g_ref, from_left, from_right, acc, tiles,
    rs_send_r, rs_recv_r, rs_send_l, rs_recv_l, ag_send_r, ag_send_l, ag_recv, w_sem, out_sem,
):
    p = lax.axis_index("col")
    rows, hidden = cot_ref.shape
    cuts = rows // unit_rows
    units = cuts * (hidden // width)
    total_rows, feats = tok_ref.shape
    groups, steps = hidden // group, cuts * group // width
    halves = steps // 2
    lag_max = 2 * (n - 1)
    has_left, has_right = p > 0, p < n - 1

    def rows_of(u, b):
        return pl.ds(pl.multiple_of(b * rows + (u % cuts) * unit_rows, unit_rows), unit_rows)

    def cols_of(u, k=0):
        return pl.ds(pl.multiple_of(k * hidden + (u // cuts) * width, width), width)

    def own_part(u, b, k):
        return part_ref[rows_of(u, b), cols_of(u, k)]

    def copy(at, send, recv, target):
        return pltpu.make_async_remote_copy(
            src_ref=at, dst_ref=at, send_sem=send, recv_sem=recv,
            device_id={"col": target}, device_id_type=MESH,
        )

    def rs_right(u, b):
        return copy(from_left.at[u, b], rs_send_r.at[u, b], rs_recv_r.at[u, b], p + 1)

    def rs_left(u, b):
        return copy(from_right.at[u, b], rs_send_l.at[u, b], rs_recv_l.at[u, b], p - 1)

    def ag_right(u, b):
        at = g_ref.at[:, rows_of(u, b), cols_of(u)]
        return copy(at, ag_send_r.at[u, b], ag_recv.at[u, b], p + 1)

    def ag_left(u, b):
        at = g_ref.at[:, rows_of(u, b), cols_of(u)]
        return copy(at, ag_send_l.at[u, b], ag_recv.at[u, b], p - 1)

    def when_unit(u, more, body):
        pl.when(jnp.logical_and(jnp.logical_and(u >= 0, u < units), more))(body)

    def relay(u, b, buffer, descriptor, arrives):
        @pl.when(arrives)
        def _():
            descriptor(u, b).wait_recv()
            for k in range(2):
                total = own_part(u, b, k) + buffer[u, b, k].astype(jnp.float32)
                buffer[u, b, k] = total.astype(buffer.dtype)

        @pl.when(jnp.logical_not(arrives))
        def _():
            for k in range(2):
                buffer[u, b, k] = own_part(u, b, k).astype(buffer.dtype)

        descriptor(u, b).start()

    def finish(u):
        for k in range(2):
            acc[k] = own_part(u, p, k)

        @pl.when(has_left)
        def _():
            rs_right(u, p).wait_recv()
            for k in range(2):
                acc[k] += from_left[u, p, k].astype(jnp.float32)

        @pl.when(has_right)
        def _():
            rs_left(u, p).wait_recv()
            for k in range(2):
                acc[k] += from_right[u, p, k].astype(jnp.float32)

        gate_pre, up_pre = acc[0], acc[1]
        sigmoid = jax.nn.sigmoid(gate_pre)
        activated = gate_pre * sigmoid
        here, at_rows, at_cols = rows_of(u, 0), rows_of(u, p), cols_of(u)
        grad_out = cot_ref[here, at_cols].astype(jnp.float32)
        hid_ref[here, at_cols] = (activated * up_pre).astype(hid_ref.dtype)
        grad_gate = grad_out * up_pre * sigmoid * (1.0 + gate_pre * (1.0 - sigmoid))
        g_ref[0, at_rows, at_cols] = grad_gate.astype(g_ref.dtype)
        g_ref[1, at_rows, at_cols] = (grad_out * activated).astype(g_ref.dtype)

        @pl.when(has_right)
        def _():
            ag_right(u, p).start()

        @pl.when(has_left)
        def _():
            ag_left(u, p).start()

    def forward_right(u, b):
        ag_right(u, b).wait_recv()
        pl.when(has_right)(lambda: ag_right(u, b).start())

    def forward_left(u, b):
        ag_left(u, b).wait_recv()
        pl.when(has_left)(lambda: ag_left(u, b).start())

    barrier = pltpu.get_barrier_semaphore()
    for here, step in ((has_left, -1), (has_right, 1)):

        @pl.when(here)
        def _():
            pl.semaphore_signal(barrier, inc=1, device_id={"col": p + step}, device_id_type=MESH)

    def weight_copy(q, k):
        return pltpu.make_async_copy(
            w_ref.at[:, pl.ds(pl.multiple_of(k * hidden + q * group, group), group)],
            weights.at[q, k], w_sem.at[q, k],
        )

    def group_cols(q, k=0):
        return pl.ds(pl.multiple_of(k * hidden + q * group, group), group)

    def piece(j, size):
        return pl.ds(pl.multiple_of(j * size, size), size)

    def forward_step(q, j):
        @pl.when(j == 0)
        def _():
            weight_copy(q, 0).wait()
            weight_copy(q, 1).wait()

        k, at = j // halves, piece(j % halves, total_rows // halves)
        part_ref[at, group_cols(q, k)] = jnp.dot(
            tok_ref[at, :], weights[q, k], preferred_element_type=jnp.float32
        )

    def out_copy(t):
        j = t % steps
        size = feats // halves // 16
        return pltpu.make_async_copy(
            tiles.at[t % 2],
            w_grad_ref.at[piece(j % halves, size), j // halves, :, group_cols(t // steps)],
            out_sem.at[t % 2],
        )

    def backward_step(t):
        q, j = t // steps, t % steps
        at = piece(j, total_rows // steps)
        share = sum(
            lax.dot_general(
                g_ref[k, at, group_cols(q)], weights[q, k], (((1,), (1,)), ((), ())),
                preferred_element_type=jnp.float32,
            )
            for k in range(2)
        )

        @pl.when(q == 0)
        def _():
            in_part_ref[at, :] = share

        @pl.when(q > 0)
        def _():
            in_part_ref[at, :] += share

        pl.when(t >= 2)(lambda: out_copy(t - 2).wait())
        tile = jnp.dot(
            tok_t[piece(j % halves, feats // halves), :], g_ref[j // halves, :, group_cols(q)],
            preferred_element_type=jnp.float32,
        )
        tiles[t % 2] = tile.astype(tiles.dtype).reshape(tiles.shape[1:])
        out_copy(t).start()

    def turn(j):
        at = piece(j, group)
        tok_t[at, :] = tok_ref[:, at].T

    def first(j, carry):
        forward_step(0, j)
        return carry

    for q in range(groups):
        for k in range(2):
            weight_copy(q, k).start()
        if q == 0:
            lax.fori_loop(0, steps, first, 0)
    pl.semaphore_wait(barrier, has_left.astype(jnp.int32) + has_right.astype(jnp.int32))

    def iteration(i, carry):
        for s in range(n - 1):
            b = n - 1 - s
            when_unit(
                i - p, p < b,
                functools.partial(relay, i - p, b, from_left, rs_right, has_left),
            )
            when_unit(
                i - (n - 1 - p), p > s,
                functools.partial(relay, i - (n - 1 - p), s, from_right, rs_left, has_right),
            )
        summed = i - jnp.maximum(p, n - 1 - p)
        when_unit(summed, True, functools.partial(finish, summed))
        for b in range(n):
            lag = max(b, n - 1 - b)
            u = i - lag - (p - b)
            when_unit(u, p > b, functools.partial(forward_right, u, b))
            u = i - lag - (b - p)
            when_unit(u, p < b, functools.partial(forward_left, u, b))
        pl.when(i + steps < units)(lambda: forward_step(i // steps + 1, i % steps))
        pl.when(i < feats // group)(lambda: turn(i))
        pl.when(i >= lag_max + steps)(lambda: backward_step(i - lag_max - steps))
        return carry

    assert feats // group <= lag_max + steps
    lax.fori_loop(0, units + lag_max + steps, iteration, 0)
    for t in range(units - 2, units):
        out_copy(t).wait()

    def drain(u, carry):
        for b in range(n):
            pl.when(p < b)(lambda: rs_right(u, b).wait_send())
            pl.when(p > b)(lambda: rs_left(u, b).wait_send())
            pl.when(jnp.logical_and(has_right, p >= b))(lambda: ag_right(u, b).wait_send())
            pl.when(jnp.logical_and(has_left, p <= b))(lambda: ag_left(u, b).wait_send())
        return carry

    lax.fori_loop(0, units, drain, 0)


def exchange(gathered, weights, cotangent, n):
    rows, hidden = cotangent.shape
    total_rows, feats = gathered.shape
    unit_rows, width, group = 64, 128, 256
    units = (rows // unit_rows) * (hidden // width)
    steps = (rows // unit_rows) * (group // width)
    vmem = pl.BlockSpec(memory_space=pltpu.VMEM)
    hbm = pl.BlockSpec(memory_space=pl.ANY)
    sem = pltpu.SemaphoreType.DMA((units, n))
    held = pltpu.VMEM((units, n, 2, unit_rows, width), jnp.bfloat16)
    return pl.pallas_call(
        functools.partial(exchange_kernel, n, unit_rows, width, group),
        out_shape=(
            jax.ShapeDtypeStruct((rows, hidden), jnp.bfloat16),
            jax.ShapeDtypeStruct((total_rows, feats), jnp.float32),
            jax.ShapeDtypeStruct((feats // 16, 2, 16, hidden), jnp.bfloat16),
        ),
        in_specs=[vmem, hbm, vmem],
        out_specs=(vmem, vmem, hbm),
        scratch_shapes=[
            pltpu.VMEM((hidden // group, 2, feats, group), jnp.bfloat16),
            pltpu.VMEM((feats, total_rows), jnp.bfloat16),
            pltpu.VMEM((total_rows, 2 * hidden), jnp.float32),
            pltpu.VMEM((2, total_rows, hidden), jnp.bfloat16),
            held, held, pltpu.VMEM((2, unit_rows, width), jnp.float32),
            pltpu.VMEM((2, feats * 2 // steps // 16, 16, group), jnp.bfloat16),
        ]
        + [sem] * 7
        + [pltpu.SemaphoreType.DMA((hidden // group, 2)), pltpu.SemaphoreType.DMA((2,))],
        compiler_params=pltpu.CompilerParams(
            collective_id=0, has_side_effects=True, vmem_limit_bytes=58 * 2**20
        ),
    )(gathered, weights, cotangent)


def tail_kernel(n, part_ref, in_grad_ref, acc, sent, got, send_sem, recv_sem):
    r = lax.axis_index("row")
    bits = n.bit_length() - 1
    rows, feats = in_grad_ref.shape
    half = feats // 2
    orders = (tuple(range(bits)), (0,) + tuple(range(bits - 1, 0, -1)))

    def own(bit):
        return (r // 2**bit) % 2

    def partner(bit):
        return r + (1 - 2 * own(bit)) * 2**bit

    def block(order, stage, e, keep):
        at = 0
        for bit in order[:stage]:
            at = at + own(bit) * 2**bit
        bit = order[stage]
        at = at + (own(bit) if keep else 1 - own(bit)) * 2**bit
        for place, bit in enumerate(order[stage + 1 :]):
            at = at + ((e >> place) & 1) * 2**bit
        return at

    def slots(stage):
        count = n >> (stage + 1)
        first = n - (n >> stage)
        return [(e, first + e) for e in range(count)]

    def copy(h, stage, slot):
        return pltpu.make_async_remote_copy(
            src_ref=sent.at[h, slot], dst_ref=got.at[h, slot],
            send_sem=send_sem.at[h, slot], recv_sem=recv_sem.at[h, slot],
            device_id={"row": partner(orders[h][stage])}, device_id_type=MESH,
        )

    def send(stage):
        for h in range(2):
            for e, slot in slots(stage):
                b = block(orders[h], stage, e, False)
                value = (part_ref if stage == 0 else acc)[
                    pl.ds(pl.multiple_of(b * rows, rows), rows), h * half : (h + 1) * half
                ]
                sent[h, slot] = value.astype(sent.dtype)
                copy(h, stage, slot).start()

    def receive(stage):
        for h in range(2):
            for e, slot in slots(stage):
                copy(h, stage, slot).wait_recv()
                b = block(orders[h], stage, e, True)
                at = (pl.ds(pl.multiple_of(b * rows, rows), rows), slice(h * half, (h + 1) * half))
                total = (part_ref if stage == 0 else acc)[at] + got[h, slot].astype(jnp.float32)
                if stage == bits - 1:
                    in_grad_ref[:, h * half : (h + 1) * half] = total.astype(in_grad_ref.dtype)
                else:
                    acc[at] = total

    barrier = pltpu.get_barrier_semaphore()
    for bit in range(bits):
        pl.semaphore_signal(barrier, inc=1, device_id={"row": partner(bit)}, device_id_type=MESH)
    pl.semaphore_wait(barrier, bits)

    for stage in range(bits):
        send(stage)
        receive(stage)
    for stage in range(bits):
        for h in range(2):
            for _, slot in slots(stage):
                copy(h, stage, slot).wait_send()


def tail(part, n):
    total_rows, feats = part.shape
    rows = total_rows // n
    vmem = pl.BlockSpec(memory_space=pltpu.VMEM)
    sem = pltpu.SemaphoreType.DMA((2, n - 1))
    held = pltpu.VMEM((2, n - 1, rows, feats // 2), jnp.bfloat16)
    return pl.pallas_call(
        functools.partial(tail_kernel, n),
        out_shape=jax.ShapeDtypeStruct((rows, feats), jnp.bfloat16),
        in_specs=[vmem],
        out_specs=vmem,
        scratch_shapes=[pltpu.VMEM((total_rows, feats), jnp.float32), held, held, sem, sem],
        compiler_params=pltpu.CompilerParams(
            collective_id=1, has_side_effects=True, vmem_limit_bytes=48 * 2**20
        ),
    )(part)


def on_device(n_row, n_col, tokens, gate_up, cotangent):
    local_feats = tokens.shape[1]
    local_hidden = gate_up.shape[2]
    gathered = lax.all_gather(tokens, "row", axis=0, tiled=True)
    weights = gate_up.reshape(local_feats, 2 * local_hidden)
    hidden, in_part, weight_grad = exchange(gathered, weights, cotangent, n_col)
    input_grad = tail(in_part, n_row)
    weight_grad = with_layout_constraint(
        jnp.transpose(weight_grad, (0, 2, 1, 3)), Layout(major_to_minor=(0, 1, 2, 3))
    )
    weight_grad = weight_grad.reshape(gate_up.shape)
    return (hidden, input_grad, weight_grad)


def solution(mesh):
    in_specs = (P("row", "col"), P("col", None, "row"), P("col", "row"))
    out_specs = (P("col", "row"), P("row", "col"), P("col", None, "row"))
    return jax.shard_map(
        functools.partial(on_device, mesh.shape["row"], mesh.shape["col"]),
        mesh=mesh, in_specs=in_specs, out_specs=out_specs, check_vma=False,
    )
```

```python
import functools

import jax
import jax.numpy as jnp
from jax import lax
from jax.experimental import pallas as pl
from jax.experimental.layout import Layout, with_layout_constraint
from jax.experimental.pallas import tpu as pltpu
from jax.sharding import PartitionSpec as P

MESH = pl.DeviceIdType.MESH


def exchange_kernel(
    n, n_row, unit_rows, width, group, *refs,
):
    blocks = refs[:n_row]
    (
    w_ref, cot_ref, hid_ref, in_part_ref, w_grad_ref, weights, tok_ref, tok_t, part_ref, g_ref, from_left, from_right, acc, tiles,
    rs_send_r, rs_recv_r, rs_send_l, rs_recv_l, ag_send_r, ag_send_l, ag_recv, w_sem, out_sem,
    tok_sem,
    ) = refs[n_row:]
    p = lax.axis_index("col")
    rows, hidden = cot_ref.shape
    cuts = rows // unit_rows
    units = cuts * (hidden // width)
    total_rows, feats = tok_ref.shape
    groups, steps = hidden // group, cuts * group // width
    halves = steps // 2
    lag_max = 2 * (n - 1)
    has_left, has_right = p > 0, p < n - 1

    def rows_of(u, b):
        return pl.ds(pl.multiple_of(b * rows + (u % cuts) * unit_rows, unit_rows), unit_rows)

    def cols_of(u, k=0):
        return pl.ds(pl.multiple_of(k * hidden + (u // cuts) * width, width), width)

    def own_part(u, b, k):
        return part_ref[rows_of(u, b), cols_of(u, k)]

    def copy(at, send, recv, target):
        return pltpu.make_async_remote_copy(
            src_ref=at, dst_ref=at, send_sem=send, recv_sem=recv,
            device_id={"col": target}, device_id_type=MESH,
        )

    def rs_right(u, b):
        return copy(from_left.at[u, b], rs_send_r.at[u, b], rs_recv_r.at[u, b], p + 1)

    def rs_left(u, b):
        return copy(from_right.at[u, b], rs_send_l.at[u, b], rs_recv_l.at[u, b], p - 1)

    def ag_right(u, b):
        at = g_ref.at[:, rows_of(u, b), cols_of(u)]
        return copy(at, ag_send_r.at[u, b], ag_recv.at[u, b], p + 1)

    def ag_left(u, b):
        at = g_ref.at[:, rows_of(u, b), cols_of(u)]
        return copy(at, ag_send_l.at[u, b], ag_recv.at[u, b], p - 1)

    def when_unit(u, more, body):
        pl.when(jnp.logical_and(jnp.logical_and(u >= 0, u < units), more))(body)

    def relay(u, b, buffer, descriptor, arrives):
        @pl.when(arrives)
        def _():
            descriptor(u, b).wait_recv()
            for k in range(2):
                total = own_part(u, b, k) + buffer[u, b, k].astype(jnp.float32)
                buffer[u, b, k] = total.astype(buffer.dtype)

        @pl.when(jnp.logical_not(arrives))
        def _():
            for k in range(2):
                buffer[u, b, k] = own_part(u, b, k).astype(buffer.dtype)

        descriptor(u, b).start()

    def finish(u):
        for k in range(2):
            acc[k] = own_part(u, p, k)

        @pl.when(has_left)
        def _():
            rs_right(u, p).wait_recv()
            for k in range(2):
                acc[k] += from_left[u, p, k].astype(jnp.float32)

        @pl.when(has_right)
        def _():
            rs_left(u, p).wait_recv()
            for k in range(2):
                acc[k] += from_right[u, p, k].astype(jnp.float32)

        gate_pre, up_pre = acc[0], acc[1]
        sigmoid = jax.nn.sigmoid(gate_pre)
        activated = gate_pre * sigmoid
        here, at_rows, at_cols = rows_of(u, 0), rows_of(u, p), cols_of(u)
        grad_out = cot_ref[here, at_cols].astype(jnp.float32)
        hid_ref[here, at_cols] = (activated * up_pre).astype(hid_ref.dtype)
        grad_gate = grad_out * up_pre * sigmoid * (1.0 + gate_pre * (1.0 - sigmoid))
        g_ref[0, at_rows, at_cols] = grad_gate.astype(g_ref.dtype)
        g_ref[1, at_rows, at_cols] = (grad_out * activated).astype(g_ref.dtype)

        @pl.when(has_right)
        def _():
            ag_right(u, p).start()

        @pl.when(has_left)
        def _():
            ag_left(u, p).start()

    def forward_right(u, b):
        ag_right(u, b).wait_recv()
        pl.when(has_right)(lambda: ag_right(u, b).start())

    def forward_left(u, b):
        ag_left(u, b).wait_recv()
        pl.when(has_left)(lambda: ag_left(u, b).start())

    barrier = pltpu.get_barrier_semaphore()
    for here, step in ((has_left, -1), (has_right, 1)):

        @pl.when(here)
        def _():
            pl.semaphore_signal(barrier, inc=1, device_id={"col": p + step}, device_id_type=MESH)

    def weight_copy(q, k):
        return pltpu.make_async_copy(
            w_ref.at[:, pl.ds(pl.multiple_of(k * hidden + q * group, group), group)],
            weights.at[q, k], w_sem.at[q, k],
        )

    def group_cols(q, k=0):
        return pl.ds(pl.multiple_of(k * hidden + q * group, group), group)

    def piece(j, size):
        return pl.ds(pl.multiple_of(j * size, size), size)

    def forward_step(q, j):
        @pl.when(j == 0)
        def _():
            weight_copy(q, 0).wait()
            weight_copy(q, 1).wait()

        k, at = j // halves, piece(j % halves, total_rows // halves)
        part_ref[at, group_cols(q, k)] = jnp.dot(
            tok_ref[at, :], weights[q, k], preferred_element_type=jnp.float32
        )

    def out_copy(t):
        j = t % steps
        size = feats // halves // 16
        return pltpu.make_async_copy(
            tiles.at[t % 2],
            w_grad_ref.at[piece(j % halves, size), j // halves, :, group_cols(t // steps)],
            out_sem.at[t % 2],
        )

    def backward_step(t):
        q, j = t // steps, t % steps
        at = piece(j, total_rows // steps)
        share = sum(
            lax.dot_general(
                g_ref[k, at, group_cols(q)], weights[q, k], (((1,), (1,)), ((), ())),
                preferred_element_type=jnp.float32,
            )
            for k in range(2)
        )

        @pl.when(q == 0)
        def _():
            in_part_ref[at, :] = share

        @pl.when(q > 0)
        def _():
            in_part_ref[at, :] += share

        pl.when(t >= 2)(lambda: out_copy(t - 2).wait())
        tile = jnp.dot(
            tok_t[piece(j % halves, feats // halves), :], g_ref[j // halves, :, group_cols(q)],
            preferred_element_type=jnp.float32,
        )
        tiles[t % 2] = tile.astype(tiles.dtype).reshape(tiles.shape[1:])
        out_copy(t).start()

    r = lax.axis_index("row")

    def block_copy(d):
        at = 0
        for bit in range(n_row.bit_length() - 1):
            mine = (r // 2**bit) % 2
            at = at + (1 - mine if (d >> bit) & 1 else mine) * 2**bit
        return pltpu.make_async_copy(
            blocks[d], tok_ref.at[piece(at, total_rows // n_row)], tok_sem.at[d]
        )

    for d in range(n_row):
        block_copy(d).start()

    def turn(j):
        at = piece(j, group)
        tok_t[at, :] = tok_ref[:, at].T

    def first(j, carry):
        forward_step(0, j)
        return carry

    for q in range(groups):
        for k in range(2):
            weight_copy(q, k).start()
        if q == 0:
            for d in range(n_row):
                block_copy(d).wait()
            lax.fori_loop(0, steps, first, 0)
    pl.semaphore_wait(barrier, has_left.astype(jnp.int32) + has_right.astype(jnp.int32))

    def iteration(i, carry):
        for s in range(n - 1):
            b = n - 1 - s
            when_unit(
                i - p, p < b,
                functools.partial(relay, i - p, b, from_left, rs_right, has_left),
            )
            when_unit(
                i - (n - 1 - p), p > s,
                functools.partial(relay, i - (n - 1 - p), s, from_right, rs_left, has_right),
            )
        summed = i - jnp.maximum(p, n - 1 - p)
        when_unit(summed, True, functools.partial(finish, summed))
        for b in range(n):
            lag = max(b, n - 1 - b)
            u = i - lag - (p - b)
            when_unit(u, p > b, functools.partial(forward_right, u, b))
            u = i - lag - (b - p)
            when_unit(u, p < b, functools.partial(forward_left, u, b))
        pl.when(i + steps < units)(lambda: forward_step(i // steps + 1, i % steps))
        pl.when(i < feats // group)(lambda: turn(i))
        pl.when(i >= lag_max + steps)(lambda: backward_step(i - lag_max - steps))
        return carry

    assert feats // group <= lag_max + steps
    lax.fori_loop(0, units + lag_max + steps, iteration, 0)
    for t in range(units - 2, units):
        out_copy(t).wait()

    def drain(u, carry):
        for b in range(n):
            pl.when(p < b)(lambda: rs_right(u, b).wait_send())
            pl.when(p > b)(lambda: rs_left(u, b).wait_send())
            pl.when(jnp.logical_and(has_right, p >= b))(lambda: ag_right(u, b).wait_send())
            pl.when(jnp.logical_and(has_left, p <= b))(lambda: ag_left(u, b).wait_send())
        return carry

    lax.fori_loop(0, units, drain, 0)


def exchange(blocks, weights, cotangent, n):
    rows, hidden = cotangent.shape
    n_row = len(blocks)
    total_rows, feats = n_row * blocks[0].shape[0], blocks[0].shape[1]
    unit_rows, width, group = 64, 128, 256
    units = (rows // unit_rows) * (hidden // width)
    steps = (rows // unit_rows) * (group // width)
    vmem = pl.BlockSpec(memory_space=pltpu.VMEM)
    hbm = pl.BlockSpec(memory_space=pl.ANY)
    sem = pltpu.SemaphoreType.DMA((units, n))
    held = pltpu.VMEM((units, n, 2, unit_rows, width), jnp.bfloat16)
    return pl.pallas_call(
        functools.partial(exchange_kernel, n, n_row, unit_rows, width, group),
        out_shape=(
            jax.ShapeDtypeStruct((rows, hidden), jnp.bfloat16),
            jax.ShapeDtypeStruct((total_rows, feats), jnp.float32),
            jax.ShapeDtypeStruct((feats // 16, 2, 16, hidden), jnp.bfloat16),
        ),
        in_specs=[hbm] * n_row + [hbm, vmem],
        out_specs=(vmem, vmem, hbm),
        scratch_shapes=[
            pltpu.VMEM((hidden // group, 2, feats, group), jnp.bfloat16),
            pltpu.VMEM((total_rows, feats), jnp.bfloat16),
            pltpu.VMEM((feats, total_rows), jnp.bfloat16),
            pltpu.VMEM((total_rows, 2 * hidden), jnp.float32),
            pltpu.VMEM((2, total_rows, hidden), jnp.bfloat16),
            held, held, pltpu.VMEM((2, unit_rows, width), jnp.float32),
            pltpu.VMEM((2, feats * 2 // steps // 16, 16, group), jnp.bfloat16),
        ]
        + [sem] * 7
        + [pltpu.SemaphoreType.DMA((hidden // group, 2)), pltpu.SemaphoreType.DMA((2,))]
        + [pltpu.SemaphoreType.DMA((n_row,))],
        compiler_params=pltpu.CompilerParams(
            collective_id=0, has_side_effects=True, vmem_limit_bytes=58 * 2**20
        ),
    )(*blocks, weights, cotangent)


def tail_kernel(n, part_ref, in_grad_ref, acc, sent, got, send_sem, recv_sem):
    r = lax.axis_index("row")
    bits = n.bit_length() - 1
    rows, feats = in_grad_ref.shape
    half = feats // 2
    orders = (tuple(range(bits)), (0,) + tuple(range(bits - 1, 0, -1)))

    def own(bit):
        return (r // 2**bit) % 2

    def partner(bit):
        return r + (1 - 2 * own(bit)) * 2**bit

    def block(order, stage, e, keep):
        at = 0
        for bit in order[:stage]:
            at = at + own(bit) * 2**bit
        bit = order[stage]
        at = at + (own(bit) if keep else 1 - own(bit)) * 2**bit
        for place, bit in enumerate(order[stage + 1 :]):
            at = at + ((e >> place) & 1) * 2**bit
        return at

    def slots(stage):
        count = n >> (stage + 1)
        first = n - (n >> stage)
        return [(e, first + e) for e in range(count)]

    def copy(h, stage, slot):
        return pltpu.make_async_remote_copy(
            src_ref=sent.at[h, slot], dst_ref=got.at[h, slot],
            send_sem=send_sem.at[h, slot], recv_sem=recv_sem.at[h, slot],
            device_id={"row": partner(orders[h][stage])}, device_id_type=MESH,
        )

    def send(stage):
        for h in range(2):
            for e, slot in slots(stage):
                b = block(orders[h], stage, e, False)
                value = (part_ref if stage == 0 else acc)[
                    pl.ds(pl.multiple_of(b * rows, rows), rows), h * half : (h + 1) * half
                ]
                sent[h, slot] = value.astype(sent.dtype)
                copy(h, stage, slot).start()

    def receive(stage):
        for h in range(2):
            for e, slot in slots(stage):
                copy(h, stage, slot).wait_recv()
                b = block(orders[h], stage, e, True)
                at = (pl.ds(pl.multiple_of(b * rows, rows), rows), slice(h * half, (h + 1) * half))
                total = (part_ref if stage == 0 else acc)[at] + got[h, slot].astype(jnp.float32)
                if stage == bits - 1:
                    in_grad_ref[:, h * half : (h + 1) * half] = total.astype(in_grad_ref.dtype)
                else:
                    acc[at] = total

    barrier = pltpu.get_barrier_semaphore()
    for bit in range(bits):
        pl.semaphore_signal(barrier, inc=1, device_id={"row": partner(bit)}, device_id_type=MESH)
    pl.semaphore_wait(barrier, bits)

    for stage in range(bits):
        send(stage)
        receive(stage)
    for stage in range(bits):
        for h in range(2):
            for _, slot in slots(stage):
                copy(h, stage, slot).wait_send()


def tail(part, n):
    total_rows, feats = part.shape
    rows = total_rows // n
    vmem = pl.BlockSpec(memory_space=pltpu.VMEM)
    sem = pltpu.SemaphoreType.DMA((2, n - 1))
    held = pltpu.VMEM((2, n - 1, rows, feats // 2), jnp.bfloat16)
    return pl.pallas_call(
        functools.partial(tail_kernel, n),
        out_shape=jax.ShapeDtypeStruct((rows, feats), jnp.bfloat16),
        in_specs=[vmem],
        out_specs=vmem,
        scratch_shapes=[pltpu.VMEM((total_rows, feats), jnp.float32), held, held, sem, sem],
        compiler_params=pltpu.CompilerParams(
            collective_id=1, has_side_effects=True, vmem_limit_bytes=48 * 2**20
        ),
    )(part)


def gather_blocks(tokens, n):
    def swapped(block, d):
        return lax.ppermute(block, "row", [(i, i ^ d) for i in range(n)])

    even = [tokens] + [swapped(tokens, d) for d in range(2, n, 2)]
    return [block for d, own in enumerate(even) for block in (own, swapped(own, 1))]


def on_device(n_row, n_col, tokens, gate_up, cotangent):
    local_feats = tokens.shape[1]
    local_hidden = gate_up.shape[2]
    blocks = gather_blocks(tokens, n_row)
    weights = gate_up.reshape(local_feats, 2 * local_hidden)
    hidden, in_part, weight_grad = exchange(blocks, weights, cotangent, n_col)
    input_grad = tail(in_part, n_row)
    weight_grad = with_layout_constraint(
        jnp.transpose(weight_grad, (0, 2, 1, 3)), Layout(major_to_minor=(0, 1, 2, 3))
    )
    weight_grad = weight_grad.reshape(gate_up.shape)
    return (hidden, input_grad, weight_grad)


def solution(mesh):
    in_specs = (P("row", "col"), P("col", None, "row"), P("col", "row"))
    out_specs = (P("col", "row"), P("row", "col"), P("col", None, "row"))
    return jax.shard_map(
        functools.partial(on_device, mesh.shape["row"], mesh.shape["col"]),
        mesh=mesh, in_specs=in_specs, out_specs=out_specs, check_vma=False,
    )
```
